32 devices in a mesh: seq: 8 (over z, y), head: 4 (over x, core).
Axes of the slice: x: 2, y: 2, z: 4, core: 2. Of those that a mesh axis runs over, the one named last changes fastest.
Arguments:
- queries: bfloat16 [2048, 2048], P('seq', 'head'), parts along dimension 1, may hold values from -6 to 6
- keys: bfloat16 [2048, 512], P('seq', 'head'), parts along dimension 1, may hold values from -6 to 6
- values: bfloat16 [2048, 512], P('seq', 'head'), parts along dimension 1, may hold values from -6 to 6
- grad_out: bfloat16 [2048, 2048], P('seq', 'head'), parts along dimension 1, may hold values from -6 to 6
- lengths: int32 [16], replicated, may hold values from 1 to 512, 2048 in all
- send_order: int32 [8, 256], replicated, may hold values from 0 to 255, each once within a row
Outputs:
- attended: float32 [2048, 2048], P('seq', 'head'), parts along dimension 1
- grad_queries: float32 [2048, 2048], P('seq', 'head'), parts along dimension 1
- grad_keys: float32 [2048, 512], P('seq', 'head'), parts along dimension 1
- grad_values: float32 [2048, 512], P('seq', 'head'), parts along dimension 1
The draws below stay inside these ranges and needn't reach their ends.
There are 4 independent parts, one for each index of `head`. The reference program is written for one: setup_inputs(seed, part) draws one part's arguments, and reference() takes and returns one part's arrays. A program takes and returns all parts, laid end to end along the dimension named above; an argument that names none is the same for every part. Nothing has to cross between parts.
Inputs may be any that keep to these rules, and one draw needn't show every extreme that they name: `lengths`: they sum to 2048; the longest is exactly 512. `send_order`: each row is a permutation of 0 to 255.
All inputs are finite; a program needn't handle non-finite values.
Results may differ from the reference program's by a relative error of at most 0.039.
Values may be sent and summed in bfloat16 or wider, within the bound.
A program may use at most 64 MiB of HBM per device.

```python
import math
import jax
import jax.numpy as jnp
import numpy as np
from jax import lax

HD = 128
QH = 4
TOK_DEV = 256
DOCS = 16
SHARDS = 8
GROUP = 32
TOKENS = 2048
LONGEST = 512


def draw_queries(key, part):
    base = jnp.clip(1.5 * jax.random.normal(jax.random.fold_in(key, 1), (TOKENS, QH, HD), jnp.float32), -6.0, 6.0)
    return base.reshape(TOKENS, QH * HD).astype(jnp.bfloat16)


def draw_keys(key, part):
    base = jnp.clip(jax.random.normal(jax.random.fold_in(key, 2), (TOKENS, HD), jnp.float32), -6.0, 6.0)
    return base.astype(jnp.bfloat16)


def draw_values(key, part):
    base = jnp.clip(jax.random.normal(jax.random.fold_in(key, 3), (TOKENS, HD), jnp.float32), -6.0, 6.0)
    return base.astype(jnp.bfloat16)


def block_scale(stream_key, extent, pieces, smallest, high):
    factor_of, own = 1.0, jax.random.fold_in(stream_key, 6)
    for dim, blocks in pieces:
        draws = jnp.exp(jax.random.uniform(jax.random.fold_in(own, dim), (blocks,), jnp.float32, smallest / len(pieces), high / len(pieces)))
        factor_of = factor_of * jnp.repeat(draws, extent[dim] // blocks).reshape([-1 if axis == dim else 1 for axis in range(len(extent))])
    return factor_of


def profile(count, total, limit, slope):
    portions = [(1 << 20) // math.isqrt(rank ** slope) + 1 for rank in range(2, count + 1)]
    rest, counts = total - limit - (count - 1), [1] * (count - 1)
    while rest > 0:
        movable = [i for i in range(count - 1) if counts[i] < limit]
        whole, remaining = sum([portions[i] for i in movable]), rest
        for i in movable:
            extra = min(limit - counts[i], max(1, remaining * portions[i] // whole), rest)
            counts[i] = counts[i] + extra
            rest = rest - extra
    return np.array([limit] + counts)


def ragged(rng, number_of, total, bound, lean):
    if number_of == 2:
        one = jax.random.randint(rng, (), max(1, total - bound), min(bound, total - 1) + 1)
        return jnp.stack([one, total - one])
    sizes = jnp.asarray(profile(number_of, total, bound, lean), jnp.int32)
    couples = (number_of - 1) // 2
    giver, taker = sizes[1:1 + 2 * couples:2], sizes[2:2 + 2 * couples:2]
    slack = jnp.minimum(giver - 1, bound - taker)
    moved = jax.random.randint(jax.random.fold_in(rng, 1), (couples,), 0, 1 << 20) % (slack + 1)
    sizes = sizes.at[1:1 + 2 * couples:2].set(giver - moved).at[2:2 + 2 * couples:2].set(taker + moved)
    return sizes[jax.random.permutation(jax.random.fold_in(rng, 2), number_of)]


def gaussian(stream_key, dims, deviation, limit, split=(), held_as=jnp.bfloat16):
    entries = jax.random.normal(stream_key, dims, jnp.float32) * deviation
    if len(split) > 0:
        entries = block_scale(stream_key, dims, split, -0.22, 0.18) * entries
    return jnp.clip(entries, min=-limit, max=limit).astype(held_as)


def setup_inputs(seed: int = 0, part: int = 0) -> dict:
    key_list = jax.random.split(jax.random.key(seed), 7)
    part_splits = jax.random.split(jax.random.fold_in(key_list[6], part), 7)
    return {
        "queries": draw_queries(jax.random.fold_in(jax.random.fold_in(key_list[6], part), 71), part),
        "keys": draw_keys(jax.random.fold_in(jax.random.fold_in(key_list[6], part), 71), part),
        "values": draw_values(jax.random.fold_in(jax.random.fold_in(key_list[6], part), 71), part),
        "grad_out": gaussian(part_splits[3], (TOKENS, QH * HD), 1.0, 6.0, ((0, 8),)),
        "lengths": ragged(key_list[4], DOCS, TOKENS, LONGEST, 2).astype(jnp.int32),
        "send_order": jax.vmap(lambda own: jax.random.permutation(own, TOK_DEV))(jax.random.split(key_list[5], SHARDS)).reshape((SHARDS, TOK_DEV)).astype(jnp.int32),
    }


masked_value = -1e+30

def doc_index(positions, bounds):
    return lax.optimization_barrier(jnp.sum((positions[:, None] >= bounds[None, :]).astype(jnp.int32), axis=1))

def reference(queries, keys, values, grad_out, lengths, send_order):
    bounds = jnp.cumsum(lengths)
    order_blocks = send_order.reshape(SHARDS, SHARDS, GROUP).transpose(1, 0, 2)
    source = (jnp.arange(SHARDS, dtype=jnp.int32)[None, :, None] * TOK_DEV + order_blocks).reshape(TOKENS).astype(jnp.int32)
    picked = jnp.take(queries, source, axis=0).reshape(TOKENS, QH, HD)
    grad_heads = grad_out.reshape(TOKENS, QH, HD)
    key_pos = jnp.arange(TOKENS, dtype=jnp.int32)
    key_doc = doc_index(key_pos, bounds)
    key_float = keys.astype(jnp.float32)
    value_float = values.astype(jnp.float32)
    score_scale = 1.0 / math.sqrt(HD)
    block_rows = math.gcd(TOKENS, 512)
    block_count = TOKENS // block_rows

    def query_block(sums, block_item):
        query_heads, grad_block, query_pos = block_item
        query_doc = doc_index(query_pos, bounds)
        allowed = ((query_doc[:, None] == key_doc[None, :]) & (key_pos[None, :] <= query_pos[:, None]))[:, None, :]
        query_float = query_heads.astype(jnp.float32)
        grad_float = grad_block.astype(jnp.float32)
        scores = jnp.where(allowed, jnp.einsum('bhd,td->bht', query_float, key_float) * score_scale, masked_value)
        row_max = lax.optimization_barrier(jnp.max(scores, axis=2))
        log_total = row_max + jnp.log(lax.optimization_barrier(jnp.sum(jnp.exp(scores - row_max[:, :, None]), axis=2)))
        weights = jnp.where(allowed, jnp.exp(scores - log_total[:, :, None]), 0.0)
        weights_low = weights.astype(jnp.bfloat16)
        attended = jnp.einsum('bht,td->bhd', weights, value_float)
        attended_low = attended.astype(jnp.bfloat16)
        out_dot = lax.optimization_barrier(jnp.sum(grad_float * attended_low.astype(jnp.float32), axis=2))
        grad_dots = jnp.einsum('bhd,td->bht', grad_float, value_float)
        score_grads = (weights * (grad_dots - out_dot[:, :, None])).astype(jnp.bfloat16)
        grads_float = score_grads.astype(jnp.float32)
        grad_query = jnp.einsum('bht,td->bhd', grads_float, key_float) * score_scale
        key_sums = sums[0] + jnp.einsum('bht,bhd->td', grads_float, query_float) * score_scale
        value_sums = sums[1] + jnp.einsum('bht,bhd->td', weights_low.astype(jnp.float32), grad_float)
        return ((key_sums, value_sums), (attended, grad_query))
    zero_sums = (jnp.zeros((TOKENS, HD), jnp.float32), jnp.zeros((TOKENS, HD), jnp.float32))
    block_items = (picked.reshape(block_count, block_rows, QH, HD), grad_heads.reshape(block_count, block_rows, QH, HD), source.reshape(block_count, block_rows))
    (key_sums, value_sums), (attended, grad_query) = lax.scan(query_block, zero_sums, block_items)
    return (attended.reshape(TOKENS, QH * HD), grad_query.reshape(TOKENS, QH * HD), key_sums, value_sums)
```

```python
import functools
import math

import jax
import jax.numpy as jnp
from jax import lax
from jax.experimental import pallas as pl
from jax.experimental.pallas import tpu as pltpu
from jax.sharding import PartitionSpec as P

MESH = pl.DeviceIdType.MESH
masked_value = -1e30


def dot_nt(a, b):
    return lax.dot_general(a, b, (((1,), (1,)), ((), ())), preferred_element_type=jnp.float32)


def dot_nn(a, b):
    return jnp.dot(a, b, preferred_element_type=jnp.float32)


def kernel(
    n,
    back,
    q_ref,
    k_ref,
    v_ref,
    g_ref,
    len_ref,
    order_ref,
    att_ref,
    gq_ref,
    gk_ref,
    gv_ref,
    kwin,
    vwin,
    gbuf,
    att_buf,
    gq_buf,
    bias,
    weights,
    gk_send,
    gv_send,
    gk_land,
    gv_land,
    kv_ssem,
    kv_rsem,
    g_ssem,
    g_rsem,
    a_ssem,
    a_rsem,
    gq_ssem,
    gq_rsem,
    gkv_ssem,
    gkv_rsem,
    own_sem,
):
    me = lax.axis_index("seq")
    tok, head_dim = k_ref.shape
    group = tok // n
    heads = q_ref.shape[1] // head_dim
    window = (back + 1) * tok
    scale = 1.0 / math.sqrt(head_dim)

    def peer(offset):
        return lax.rem(me + offset, n)

    def remote(src, dst, ssem, rsem, target):
        return pltpu.make_async_remote_copy(
            src_ref=src,
            dst_ref=dst,
            send_sem=ssem,
            recv_sem=rsem,
            device_id={"seq": target},
            device_id_type=MESH,
        )

    def halo_in(b):
        rows = pl.ds((back - b) * tok, tok)
        target = peer(b)
        return (
            remote(k_ref, kwin.at[rows], kv_ssem.at[0, b - 1], kv_rsem.at[0, b - 1], target),
            remote(v_ref, vwin.at[rows], kv_ssem.at[1, b - 1], kv_rsem.at[1, b - 1], target),
        )

    def halo_out(b):
        target = peer(n - b)
        return (
            remote(
                gk_send.at[b - 1],
                gk_land.at[b - 1],
                gkv_ssem.at[0, b - 1],
                gkv_rsem.at[0, b - 1],
                target,
            ),
            remote(
                gv_send.at[b - 1],
                gv_land.at[b - 1],
                gkv_ssem.at[1, b - 1],
                gkv_rsem.at[1, b - 1],
                target,
            ),
        )

    def spread(src, dst, ssem, rsem, offset):
        target = peer(offset)
        return remote(src.at[target], dst.at[me], ssem.at[offset], rsem.at[offset], target)

    barrier = pltpu.get_barrier_semaphore()
    for offset in range(1, n):
        pl.semaphore_signal(
            barrier, inc=1, device_id={"seq": peer(offset)}, device_id_type=MESH
        )

    own_grad = pltpu.make_async_copy(g_ref.at[me], gbuf.at[me], own_sem.at[0])
    own_grad.start()
    kwin[back * tok :, :] = k_ref[...]
    vwin[back * tok :, :] = v_ref[...]
    for b in range(1, back + 1):

        @pl.when(me < b)
        def _():
            kwin[(back - b) * tok : (back - b + 1) * tok, :] = jnp.zeros((tok, head_dim), kwin.dtype)
            vwin[(back - b) * tok : (back - b + 1) * tok, :] = jnp.zeros((tok, head_dim), vwin.dtype)

    pl.semaphore_wait(barrier, n - 1)
    for b in range(1, back + 1):

        @pl.when(me + b < n)
        def _():
            for copy in halo_in(b):
                copy.start()

    for offset in range(1, n):
        spread(g_ref, gbuf, g_ssem, g_rsem, offset).start()

    order = order_ref[pl.ds(me, 1), :]
    one_hot = (lax.broadcasted_iota(jnp.int32, (tok, tok), 0) == order).astype(jnp.float32)
    picked = dot_nn(one_hot.T.astype(jnp.bfloat16), q_ref[...]).astype(jnp.bfloat16)
    query_pos = order + me * tok
    start = jnp.zeros_like(query_pos)
    bound = jnp.int32(0)
    for d in range(len_ref.shape[0]):
        bound = bound + len_ref[d]
        start = jnp.where(query_pos >= bound, bound, start)
    key_pos = lax.broadcasted_iota(jnp.int32, (window, tok), 0) + (me - back) * tok
    allowed = (key_pos >= start) & (key_pos <= query_pos)
    bias[...] = jnp.where(allowed, 0.0, masked_value)

    for b in range(1, back + 1):

        @pl.when(me >= b)
        def _():
            for copy in halo_in(b):
                copy.wait_recv()

    key_all = kwin[...]
    value_all = vwin[...]
    key_t = key_all.astype(jnp.float32).T.astype(jnp.bfloat16)
    value_t = value_all.astype(jnp.float32).T.astype(jnp.bfloat16)
    exponent = scale * math.log2(math.e)

    att_cols = []
    for h in range(heads):
        cols = slice(h * head_dim, (h + 1) * head_dim)
        scores = dot_nt(key_all, picked[:, cols]) + bias[...]
        row_max = jnp.max(scores, axis=0, keepdims=True)
        exps = jnp.exp2((scores - row_max) * exponent)
        weight = exps * (1.0 / jnp.sum(exps, axis=0, keepdims=True))
        weights[h] = weight
        att_t = dot_nn(value_t, weight.astype(jnp.bfloat16))
        att_low = att_t.T
        att_cols.append(att_t.astype(jnp.bfloat16).astype(jnp.float32))
        att_buf[:, :, cols] = att_low.reshape(n, group, head_dim).astype(jnp.bfloat16)
    own_att = pltpu.make_async_copy(att_buf.at[me], att_ref.at[me], own_sem.at[1])
    own_att.start()
    for offset in range(1, n):
        spread(att_buf, att_ref, a_ssem, a_rsem, offset).start()

    own_grad.wait()
    for offset in range(1, n):
        spread(g_ref, gbuf, g_ssem, g_rsem, offset).wait_recv()

    key_sum = None
    for h in range(heads):
        cols = slice(h * head_dim, (h + 1) * head_dim)
        grad_float = gbuf[:, :, cols].astype(jnp.float32).reshape(tok, head_dim)
        grad = grad_float.astype(jnp.bfloat16)
        out_dot = jnp.sum(grad_float.T * att_cols[h], axis=0, keepdims=True)
        weight = weights[h]
        score_grads = (weight * (dot_nt(value_all, grad) - out_dot)).astype(jnp.bfloat16)
        query_grad = (dot_nn(key_t, score_grads) * scale).T
        gq_buf[:, :, cols] = query_grad.reshape(n, group, head_dim).astype(jnp.bfloat16)
        key_term = dot_nn(score_grads, picked[:, cols])
        value_term = dot_nn(weight.astype(jnp.bfloat16), grad)
        key_sum = key_term if key_sum is None else key_sum + key_term
        value_sum = value_term if h == 0 else value_sum + value_term

    own_gq = pltpu.make_async_copy(gq_buf.at[me], gq_ref.at[me], own_sem.at[2])
    own_gq.start()
    for offset in range(1, n):
        spread(gq_buf, gq_ref, gq_ssem, gq_rsem, offset).start()
    key_sum = key_sum * scale
    for b in range(1, back + 1):
        rows = slice((back - b) * tok, (back - b + 1) * tok)
        gk_send[b - 1] = key_sum[rows, :].astype(jnp.bfloat16)
        gv_send[b - 1] = value_sum[rows, :].astype(jnp.bfloat16)

        @pl.when(me >= b)
        def _():
            for copy in halo_out(b):
                copy.start()

    gk_ref[...] = key_sum[back * tok :, :]
    gv_ref[...] = value_sum[back * tok :, :]
    for b in range(1, back + 1):

        @pl.when(me + b < n)
        def _():
            for copy in halo_in(b):
                copy.wait_send()
            for copy in halo_out(b):
                copy.wait_recv()
            gk_ref[...] += gk_land[b - 1].astype(jnp.float32)
            gv_ref[...] += gv_land[b - 1].astype(jnp.float32)

        @pl.when(me >= b)
        def _():
            for copy in halo_out(b):
                copy.wait_send()

    own_att.wait()
    own_gq.wait()
    for offset in range(1, n):
        spread(g_ref, gbuf, g_ssem, g_rsem, offset).wait_send()
        spread(att_buf, att_ref, a_ssem, a_rsem, offset).wait()
        spread(gq_buf, gq_ref, gq_ssem, gq_rsem, offset).wait()


def per_device(n, queries, keys, values, grad_out, lengths, send_order):
    tok, head_dim = keys.shape
    width = queries.shape[1]
    heads = width // head_dim
    group = tok // n
    longest = n * tok // 4
    back = min(n - 1, -(-(longest - 1) // tok))
    window = (back + 1) * tok
    flops = 2 * tok * heads * window * head_dim * 5
    vmem = pl.BlockSpec(memory_space=pltpu.VMEM)
    hbm = pl.BlockSpec(memory_space=pl.ANY)
    smem = pl.BlockSpec(memory_space=pltpu.SMEM)
    dma = pltpu.SemaphoreType.DMA
    att, gq, gk, gv = pl.pallas_call(
        functools.partial(kernel, n, back),
        out_shape=(
            jax.ShapeDtypeStruct((n, group, width), jnp.bfloat16),
            jax.ShapeDtypeStruct((n, group, width), jnp.bfloat16),
            jax.ShapeDtypeStruct((tok, head_dim), jnp.float32),
            jax.ShapeDtypeStruct((tok, head_dim), jnp.float32),
        ),
        in_specs=[vmem, vmem, vmem, hbm, smem, vmem],
        out_specs=(hbm, hbm, vmem, vmem),
        scratch_shapes=[
            pltpu.VMEM((window, head_dim), jnp.bfloat16),
            pltpu.VMEM((window, head_dim), jnp.bfloat16),
            pltpu.VMEM((n, group, width), jnp.bfloat16),
            pltpu.VMEM((n, group, width), jnp.bfloat16),
            pltpu.VMEM((n, group, width), jnp.bfloat16),
            pltpu.VMEM((window, tok), jnp.float32),
            pltpu.VMEM((heads, window, tok), jnp.float32),
            pltpu.VMEM((back, tok, head_dim), jnp.bfloat16),
            pltpu.VMEM((back, tok, head_dim), jnp.bfloat16),
            pltpu.VMEM((back, tok, head_dim), jnp.bfloat16),
            pltpu.VMEM((back, tok, head_dim), jnp.bfloat16),
            dma((2, back)),
            dma((2, back)),
            dma((n,)),
            dma((n,)),
            dma((n,)),
            dma((n,)),
            dma((n,)),
            dma((n,)),
            dma((2, back)),
            dma((2, back)),
            dma((3,)),
        ],
        compiler_params=pltpu.CompilerParams(
            collective_id=0, has_side_effects=True, vmem_limit_bytes=48 * 1024 * 1024
        ),
        cost_estimate=pl.CostEstimate(
            flops=flops, bytes_accessed=6 * tok * width, transcendentals=tok * heads * window
        ),
    )(queries, keys, values, grad_out.reshape(n, group, width), lengths, send_order)
    return (
        att.reshape(tok, width).astype(jnp.float32),
        gq.reshape(tok, width).astype(jnp.float32),
        gk,
        gv,
    )


def solution(mesh):
    placed = (P("seq", "head"), P("seq", "head"), P("seq", "head"), P("seq", "head"), P(), P())
    return jax.shard_map(
        functools.partial(per_device, mesh.shape["seq"]),
        mesh=mesh,
        in_specs=placed,
        out_specs=(P("seq", "head"), P("seq", "head"), P("seq", "head"), P("seq", "head")),
        check_vma=False,
    )
```

```python
import functools
import math

import jax
import jax.numpy as jnp
from jax import lax
from jax.experimental import pallas as pl
from jax.experimental.pallas import tpu as pltpu
from jax.sharding import PartitionSpec as P

MESH = pl.DeviceIdType.MESH
masked_value = -1e30


def dot_nt(a, b):
    return lax.dot_general(a, b, (((1,), (1,)), ((), ())), preferred_element_type=jnp.float32)


def dot_nn(a, b):
    return jnp.dot(a, b, preferred_element_type=jnp.float32)


def kernel(
    n,
    back,
    q_hbm,
    k_ref,
    v_ref,
    g_ref,
    len_hbm,
    order_hbm,
    att_ref,
    gq_ref,
    gk_ref,
    gv_ref,
    q_ref,
    len_ref,
    order_ref,
    kwin,
    vwin,
    gbuf,
    att_buf,
    gq_buf,
    bias,
    weights,
    gk_send,
    gv_send,
    gk_land,
    gv_land,
    kv_ssem,
    kv_rsem,
    g_ssem,
    g_rsem,
    a_ssem,
    a_rsem,
    gq_ssem,
    gq_rsem,
    gkv_ssem,
    gkv_rsem,
    own_sem,
):
    me = lax.axis_index("seq")
    tok, head_dim = k_ref.shape
    group = tok // n
    parts = a_ssem.shape[0]
    heads = q_ref.shape[1] // head_dim
    window = (back + 1) * tok
    scale = 1.0 / math.sqrt(head_dim)

    def peer(offset):
        return lax.rem(me + offset, n)

    def remote(src, dst, ssem, rsem, target):
        return pltpu.make_async_remote_copy(
            src_ref=src,
            dst_ref=dst,
            send_sem=ssem,
            recv_sem=rsem,
            device_id={"seq": target},
            device_id_type=MESH,
        )

    def halo_in(b):
        rows = pl.ds((back - b) * tok, tok)
        target = peer(b)
        return (
            remote(k_ref, kwin.at[rows], kv_ssem.at[0, b - 1], kv_rsem.at[0, b - 1], target),
            remote(v_ref, vwin.at[rows], kv_ssem.at[1, b - 1], kv_rsem.at[1, b - 1], target),
        )

    def halo_out(b):
        target = peer(n - b)
        return (
            remote(
                gk_send.at[b - 1],
                gk_land.at[b - 1],
                gkv_ssem.at[0, b - 1],
                gkv_rsem.at[0, b - 1],
                target,
            ),
            remote(
                gv_send.at[b - 1],
                gv_land.at[b - 1],
                gkv_ssem.at[1, b - 1],
                gkv_rsem.at[1, b - 1],
                target,
            ),
        )

    def spread(src, dst, ssem, rsem, offset):
        target = peer(offset)
        return remote(src.at[target], dst.at[me], ssem.at[offset], rsem.at[offset], target)

    def spread_part(src, dst, ssem, rsem, part, offset):
        target = peer(offset)
        width = heads // parts * head_dim
        cols = pl.ds(part * width, width)
        return remote(
            src.at[target, :, cols],
            dst.at[me, :, cols],
            ssem.at[part, offset],
            rsem.at[part, offset],
            target,
        )

    barrier = pltpu.get_barrier_semaphore()
    for offset in range(1, n):
        pl.semaphore_signal(
            barrier, inc=1, device_id={"seq": peer(offset)}, device_id_type=MESH
        )

    own_rows = pl.ds(back * tok, tok)
    local = [
        pltpu.make_async_copy(order_hbm, order_ref, own_sem.at[0]),
        pltpu.make_async_copy(len_hbm, len_ref, own_sem.at[1]),
        pltpu.make_async_copy(q_hbm, q_ref, own_sem.at[2]),
        pltpu.make_async_copy(k_ref, kwin.at[own_rows], own_sem.at[3]),
        pltpu.make_async_copy(v_ref, vwin.at[own_rows], own_sem.at[4]),
        pltpu.make_async_copy(g_ref.at[me], gbuf.at[me], own_sem.at[5]),
    ]
    for copy in local:
        copy.start()
    for b in range(1, back + 1):

        @pl.when(me < b)
        def _():
            kwin[(back - b) * tok : (back - b + 1) * tok, :] = jnp.zeros((tok, head_dim), kwin.dtype)
            vwin[(back - b) * tok : (back - b + 1) * tok, :] = jnp.zeros((tok, head_dim), vwin.dtype)

    pl.semaphore_wait(barrier, n - 1)
    for b in range(1, back + 1):

        @pl.when(me + b < n)
        def _():
            for copy in halo_in(b):
                copy.start()

    for offset in range(1, n):

        @pl.when(peer(offset) < me)
        def _():
            spread(g_ref, gbuf, g_ssem, g_rsem, offset).start()

    for copy in local:
        copy.wait()

    order = order_ref[pl.ds(me, 1), :]
    one_hot = (lax.broadcasted_iota(jnp.int32, (tok, tok), 0) == order).astype(jnp.float32)
    picked = dot_nn(one_hot.T.astype(jnp.bfloat16), q_ref[...]).astype(jnp.bfloat16)
    query_pos = order + me * tok
    start = jnp.zeros_like(query_pos)
    bound = jnp.int32(0)
    for d in range(len_ref.shape[0]):
        bound = bound + len_ref[d]
        start = jnp.where(query_pos >= bound, bound, start)
    key_pos = lax.broadcasted_iota(jnp.int32, (window, tok), 0) + (me - back) * tok
    allowed = (key_pos >= start) & (key_pos <= query_pos)
    bias[...] = jnp.where(allowed, 0.0, masked_value)

    for b in range(1, back + 1):

        @pl.when(me + b < n)
        def _():
            for copy in halo_in(b):
                copy.wait_send()

    for offset in range(1, n):

        @pl.when(peer(offset) > me)
        def _():
            spread(g_ref, gbuf, g_ssem, g_rsem, offset).start()

    for b in range(1, back + 1):

        @pl.when(me >= b)
        def _():
            for copy in halo_in(b):
                copy.wait_recv()

    key_all = kwin[...]
    value_all = vwin[...]
    key_t = key_all.astype(jnp.float32).T.astype(jnp.bfloat16)
    value_t = value_all.astype(jnp.float32).T.astype(jnp.bfloat16)
    exponent = scale * math.log2(math.e)

    att_cols = []
    for h in range(heads):
        cols = slice(h * head_dim, (h + 1) * head_dim)
        scores = dot_nt(key_all, picked[:, cols]) + bias[...]
        row_max = jnp.max(scores, axis=0, keepdims=True)
        exps = jnp.exp2((scores - row_max) * exponent)
        weight = exps * (1.0 / jnp.sum(exps, axis=0, keepdims=True))
        weights[h] = weight
        att_t = dot_nn(value_t, weight.astype(jnp.bfloat16))
        att_low = att_t.T
        att_cols.append(att_t.astype(jnp.bfloat16).astype(jnp.float32))
        att_buf[:, :, cols] = att_low.reshape(n, group, head_dim).astype(jnp.bfloat16)
        part = (h + 1) * parts // heads - 1
        if (h + 1) * parts % heads == 0:
            for offset in range(1, n):
                spread_part(att_buf, att_ref, a_ssem, a_rsem, part, offset).start()
    own_att = pltpu.make_async_copy(att_buf.at[me], att_ref.at[me], own_sem.at[6])
    own_att.start()

    for offset in range(1, n):
        spread(g_ref, gbuf, g_ssem, g_rsem, offset).wait_recv()

    key_sum = None
    for h in range(heads):
        cols = slice(h * head_dim, (h + 1) * head_dim)
        grad_float = gbuf[:, :, cols].astype(jnp.float32).reshape(tok, head_dim)
        grad = grad_float.astype(jnp.bfloat16)
        out_dot = jnp.sum(grad_float.T * att_cols[h], axis=0, keepdims=True)
        weight = weights[h]
        score_grads = (weight * (dot_nt(value_all, grad) - out_dot)).astype(jnp.bfloat16)
        query_grad = (dot_nn(key_t, score_grads) * scale).T
        gq_buf[:, :, cols] = query_grad.reshape(n, group, head_dim).astype(jnp.bfloat16)
        part = (h + 1) * parts // heads - 1
        if (h + 1) * parts % heads == 0:
            for offset in range(1, n):
                spread_part(gq_buf, gq_ref, gq_ssem, gq_rsem, part, offset).start()
        key_term = dot_nn(score_grads, picked[:, cols])
        value_term = dot_nn(weight.astype(jnp.bfloat16), grad)
        key_sum = key_term if key_sum is None else key_sum + key_term
        value_sum = value_term if h == 0 else value_sum + value_term

    key_sum = key_sum * scale
    for b in range(1, back + 1):
        rows = slice((back - b) * tok, (back - b + 1) * tok)
        gk_send[b - 1] = key_sum[rows, :].astype(jnp.bfloat16)
        gv_send[b - 1] = value_sum[rows, :].astype(jnp.bfloat16)

        @pl.when(me >= b)
        def _():
            for copy in halo_out(b):
                copy.start()

    own_gq = pltpu.make_async_copy(gq_buf.at[me], gq_ref.at[me], own_sem.at[7])
    own_gq.start()
    gk_ref[...] = key_sum[back * tok :, :]
    gv_ref[...] = value_sum[back * tok :, :]
    for b in range(1, back + 1):

        @pl.when(me + b < n)
        def _():
            for copy in halo_out(b):
                copy.wait_recv()
            gk_ref[...] += gk_land[b - 1].astype(jnp.float32)
            gv_ref[...] += gv_land[b - 1].astype(jnp.float32)

        @pl.when(me >= b)
        def _():
            for copy in halo_out(b):
                copy.wait_send()

    own_att.wait()
    own_gq.wait()
    for offset in range(1, n):
        spread(g_ref, gbuf, g_ssem, g_rsem, offset).wait_send()
        for part in range(parts):
            spread_part(att_buf, att_ref, a_ssem, a_rsem, part, offset).wait()
            spread_part(gq_buf, gq_ref, gq_ssem, gq_rsem, part, offset).wait()


def widen(att_ref, gq_ref, gk_ref, gv_ref, att_out, gq_out, gk_out, gv_out):
    att_out[...] = att_ref[...].astype(jnp.float32)
    gq_out[...] = gq_ref[...].astype(jnp.float32)
    gk_out[...] = gk_ref[...]
    gv_out[...] = gv_ref[...]


def per_device(n, queries, keys, values, grad_out, lengths, send_order):
    tok, head_dim = keys.shape
    width = queries.shape[1]
    heads = width // head_dim
    group = tok // n
    longest = n * tok // 4
    back = min(n - 1, -(-(longest - 1) // tok))
    window = (back + 1) * tok
    flops = 2 * tok * heads * window * head_dim * 5
    vmem = pl.BlockSpec(memory_space=pltpu.VMEM)
    hbm = pl.BlockSpec(memory_space=pltpu.HBM)
    parts = math.gcd(heads, 2)
    vmem_limit = 62 * 1024 * 1024
    dma = pltpu.SemaphoreType.DMA
    att, gq, gk, gv = pl.pallas_call(
        functools.partial(kernel, n, back),
        out_shape=(
            jax.ShapeDtypeStruct((n, group, width), jnp.bfloat16),
            jax.ShapeDtypeStruct((n, group, width), jnp.bfloat16),
            jax.ShapeDtypeStruct((tok, head_dim), jnp.float32),
            jax.ShapeDtypeStruct((tok, head_dim), jnp.float32),
        ),
        in_specs=[hbm] * 6,
        out_specs=(hbm, hbm, vmem, vmem),
        scratch_shapes=[
            pltpu.VMEM((tok, width), jnp.bfloat16),
            pltpu.SMEM(lengths.shape, jnp.int32),
            pltpu.VMEM(send_order.shape, jnp.int32),
            pltpu.VMEM((window, head_dim), jnp.bfloat16),
            pltpu.VMEM((window, head_dim), jnp.bfloat16),
            pltpu.VMEM((n, group, width), jnp.bfloat16),
            pltpu.VMEM((n, group, width), jnp.bfloat16),
            pltpu.VMEM((n, group, width), jnp.bfloat16),
            pltpu.VMEM((window, tok), jnp.float32),
            pltpu.VMEM((heads, window, tok), jnp.float32),
            pltpu.VMEM((back, tok, head_dim), jnp.bfloat16),
            pltpu.VMEM((back, tok, head_dim), jnp.bfloat16),
            pltpu.VMEM((back, tok, head_dim), jnp.bfloat16),
            pltpu.VMEM((back, tok, head_dim), jnp.bfloat16),
            dma((2, back)),
            dma((2, back)),
            dma((n,)),
            dma((n,)),
            dma((parts, n)),
            dma((parts, n)),
            dma((parts, n)),
            dma((parts, n)),
            dma((2, back)),
            dma((2, back)),
            dma((8,)),
        ],
        compiler_params=pltpu.CompilerParams(
            collective_id=0, has_side_effects=True, vmem_limit_bytes=vmem_limit
        ),
        cost_estimate=pl.CostEstimate(
            flops=flops, bytes_accessed=6 * tok * width, transcendentals=tok * heads * window
        ),
    )(queries, keys, values, grad_out.reshape(n, group, width), lengths, send_order)
    steps = 2
    wide = pl.BlockSpec((n // steps, group, width), lambda i: (i, 0, 0))
    narrow = pl.BlockSpec((tok // steps, head_dim), lambda i: (i, 0))
    blocks = (wide, wide, narrow, narrow)
    att, gq, gk, gv = pl.pallas_call(
        widen,
        out_shape=(
            jax.ShapeDtypeStruct((n, group, width), jnp.float32),
            jax.ShapeDtypeStruct((n, group, width), jnp.float32),
            jax.ShapeDtypeStruct((tok, head_dim), jnp.float32),
            jax.ShapeDtypeStruct((tok, head_dim), jnp.float32),
        ),
        grid=(steps,),
        in_specs=blocks,
        out_specs=blocks,
        compiler_params=pltpu.CompilerParams(vmem_limit_bytes=vmem_limit),
    )(att, gq, gk, gv)
    return (att.reshape(tok, width), gq.reshape(tok, width), gk, gv)


def solution(mesh):
    placed = (P("seq", "head"), P("seq", "head"), P("seq", "head"), P("seq", "head"), P(), P())
    return jax.shard_map(
        functools.partial(per_device, mesh.shape["seq"]),
        mesh=mesh,
        in_specs=placed,
        out_specs=(P("seq", "head"), P("seq", "head"), P("seq", "head"), P("seq", "head")),
        check_vma=False,
    )
```

```python
import functools
import math

import jax
import jax.numpy as jnp
from jax import lax
from jax.experimental import pallas as pl
from jax.experimental.pallas import tpu as pltpu
from jax.sharding import PartitionSpec as P

MESH = pl.DeviceIdType.MESH
masked_value = -1e30


def dot_nt(a, b):
    return lax.dot_general(a, b, (((1,), (1,)), ((), ())), preferred_element_type=jnp.float32)


def dot_nn(a, b):
    return jnp.dot(a, b, preferred_element_type=jnp.float32)


def kernel(
    n,
    back,
    q_hbm,
    k_ref,
    v_ref,
    g_ref,
    len_hbm,
    order_hbm,
    att_ref,
    gq_ref,
    gk_ref,
    gv_ref,
    q_ref,
    len_ref,
    order_ref,
    kwin,
    vwin,
    gbuf,
    att_buf,
    gq_buf,
    bias,
    weights,
    gk_send,
    gv_send,
    gk_land,
    gv_land,
    kv_ssem,
    kv_rsem,
    g_ssem,
    g_rsem,
    a_ssem,
    a_rsem,
    gq_ssem,
    gq_rsem,
    gkv_ssem,
    gkv_rsem,
    own_sem,
):
    me = lax.axis_index("seq")
    tok, head_dim = k_ref.shape
    group = tok // n
    parts = a_ssem.shape[0]
    heads = q_ref.shape[1] // head_dim
    window = (back + 1) * tok
    scale = 1.0 / math.sqrt(head_dim)

    def peer(offset):
        return lax.rem(me + offset, n)

    def remote(src, dst, ssem, rsem, target):
        return pltpu.make_async_remote_copy(
            src_ref=src,
            dst_ref=dst,
            send_sem=ssem,
            recv_sem=rsem,
            device_id={"seq": target},
            device_id_type=MESH,
        )

    relay = back == 2 and n % 2 == 0
    odd = lax.rem(me, 2)
    partner = me + 1 - 2 * odd

    def halo_in(b):
        rows = pl.ds((back - b) * tok, tok)
        target = partner if relay and b == 1 else peer(b)
        return (
            remote(k_ref, kwin.at[rows], kv_ssem.at[0, b - 1], kv_rsem.at[0, b - 1], target),
            remote(v_ref, vwin.at[rows], kv_ssem.at[1, b - 1], kv_rsem.at[1, b - 1], target),
        )

    def halo_forward():
        old, new = pl.ds(0, tok), pl.ds(tok, tok)
        return (
            remote(kwin.at[old], kwin.at[new], kv_ssem.at[0, 0], kv_rsem.at[0, 0], partner),
            remote(vwin.at[old], vwin.at[new], kv_ssem.at[1, 0], kv_rsem.at[1, 0], partner),
        )

    def halo_out(b):
        target = partner if relay and b == 1 else peer(n - b)
        return (
            remote(
                gk_send.at[b - 1],
                gk_land.at[b - 1],
                gkv_ssem.at[0, b - 1],
                gkv_rsem.at[0, b - 1],
                target,
            ),
            remote(
                gv_send.at[b - 1],
                gv_land.at[b - 1],
                gkv_ssem.at[1, b - 1],
                gkv_rsem.at[1, b - 1],
                target,
            ),
        )

    def spread(src, dst, ssem, rsem, offset):
        target = peer(offset)
        return remote(src.at[target], dst.at[me], ssem.at[offset], rsem.at[offset], target)

    def spread_part(src, dst, ssem, rsem, part, offset):
        target = peer(offset)
        width = heads // parts * head_dim
        cols = pl.ds(part * width, width)
        return remote(
            src.at[target, :, cols],
            dst.at[me, :, cols],
            ssem.at[part, offset],
            rsem.at[part, offset],
            target,
        )

    barrier = pltpu.get_barrier_semaphore()
    for offset in range(1, n):
        pl.semaphore_signal(
            barrier, inc=1, device_id={"seq": peer(offset)}, device_id_type=MESH
        )

    own_rows = pl.ds(back * tok, tok)
    local = [
        pltpu.make_async_copy(order_hbm, order_ref, own_sem.at[0]),
        pltpu.make_async_copy(len_hbm, len_ref, own_sem.at[1]),
        pltpu.make_async_copy(q_hbm, q_ref, own_sem.at[2]),
        pltpu.make_async_copy(k_ref, kwin.at[own_rows], own_sem.at[3]),
        pltpu.make_async_copy(v_ref, vwin.at[own_rows], own_sem.at[4]),
        pltpu.make_async_copy(g_ref.at[me], gbuf.at[me], own_sem.at[5]),
    ]
    for copy in local:
        copy.start()
    for b in range(1, back + 1):

        @pl.when(me < b)
        def _():
            kwin[(back - b) * tok : (back - b + 1) * tok, :] = jnp.zeros((tok, head_dim), kwin.dtype)
            vwin[(back - b) * tok : (back - b + 1) * tok, :] = jnp.zeros((tok, head_dim), vwin.dtype)

    pl.semaphore_wait(barrier, n - 1)
    for b in range(back, 0, -1):

        @pl.when((odd == 0) if relay and b == 1 else (me + b < n))
        def _():
            for copy in halo_in(b):
                copy.start()

    for offset in range(1, n):

        @pl.when(peer(offset) < me)
        def _():
            spread(g_ref, gbuf, g_ssem, g_rsem, offset).start()

    for copy in local:
        copy.wait()

    order = order_ref[pl.ds(me, 1), :]
    one_hot = (lax.broadcasted_iota(jnp.int32, (tok, tok), 0) == order).astype(jnp.float32)
    picked = dot_nn(one_hot.T.astype(jnp.bfloat16), q_ref[...]).astype(jnp.bfloat16)
    query_pos = order + me * tok
    start = jnp.zeros_like(query_pos)
    bound = jnp.int32(0)
    for d in range(len_ref.shape[0]):
        bound = bound + len_ref[d]
        start = jnp.where(query_pos >= bound, bound, start)
    key_pos = lax.broadcasted_iota(jnp.int32, (window, tok), 0) + (me - back) * tok
    allowed = (key_pos >= start) & (key_pos <= query_pos)
    bias[...] = jnp.where(allowed, 0.0, masked_value)

    if relay:

        @pl.when(me >= 2)
        def _():
            for copy, onward in zip(halo_in(2), halo_forward()):
                copy.wait_recv()

                @pl.when(odd == 1)
                def _():
                    onward.start()

    for b in range(1, back + 1):

        @pl.when((odd == 0) if relay and b == 1 else (me + b < n))
        def _():
            for copy in halo_in(b):
                copy.wait_send()

    for offset in range(1, n):

        @pl.when(peer(offset) > me)
        def _():
            spread(g_ref, gbuf, g_ssem, g_rsem, offset).start()

    for b in range(1, 2 if relay else back + 1):

        @pl.when(me >= b)
        def _():
            for copy in halo_in(b):
                copy.wait_recv()

    key_all = kwin[...]
    value_all = vwin[...]
    key_t = key_all.astype(jnp.float32).T.astype(jnp.bfloat16)
    value_t = value_all.astype(jnp.float32).T.astype(jnp.bfloat16)
    exponent = scale * math.log2(math.e)

    att_cols = []
    for h in range(heads):
        cols = slice(h * head_dim, (h + 1) * head_dim)
        scores = dot_nt(key_all, picked[:, cols]) + bias[...]
        row_max = jnp.max(scores, axis=0, keepdims=True)
        exps = jnp.exp2((scores - row_max) * exponent)
        weight = exps * (1.0 / jnp.sum(exps, axis=0, keepdims=True))
        weights[h] = weight
        att_t = dot_nn(value_t, weight.astype(jnp.bfloat16))
        att_low = att_t.T
        att_cols.append(att_t.astype(jnp.bfloat16).astype(jnp.float32))
        att_buf[:, :, cols] = att_low.reshape(n, group, head_dim).astype(jnp.bfloat16)
        part = (h + 1) * parts // heads - 1
        if (h + 1) * parts % heads == 0:
            for offset in range(1, n):
                spread_part(att_buf, att_ref, a_ssem, a_rsem, part, offset).start()
    own_att = pltpu.make_async_copy(att_buf.at[me], att_ref.at[me], own_sem.at[6])
    own_att.start()

    for offset in range(1, n):
        spread(g_ref, gbuf, g_ssem, g_rsem, offset).wait_recv()

    def send_query_grads(part):
        for h in range(part * heads // parts, (part + 1) * heads // parts):
            query_grad = (dot_nn(key_t, score_grads[h]) * scale).T
            cols = slice(h * head_dim, (h + 1) * head_dim)
            gq_buf[:, :, cols] = query_grad.reshape(n, group, head_dim).astype(jnp.bfloat16)
        for offset in range(1, n):
            spread_part(gq_buf, gq_ref, gq_ssem, gq_rsem, part, offset).start()

    score_grads = []
    for h in range(heads):
        cols = slice(h * head_dim, (h + 1) * head_dim)
        grad_float = gbuf[:, :, cols].astype(jnp.float32).reshape(tok, head_dim)
        grad = grad_float.astype(jnp.bfloat16)
        out_dot = jnp.sum(grad_float.T * att_cols[h], axis=0, keepdims=True)
        weight = weights[h]
        score_grads.append((weight * (dot_nt(value_all, grad) - out_dot)).astype(jnp.bfloat16))
        key_term = dot_nn(score_grads[h], picked[:, cols])
        value_term = dot_nn(weight.astype(jnp.bfloat16), grad)
        key_sum = key_term if h == 0 else key_sum + key_term
        value_sum = value_term if h == 0 else value_sum + value_term
        if h + 1 < heads and (h + 1) * parts % heads == 0:
            send_query_grads((h + 1) * parts // heads - 1)

    key_sum = key_sum * scale

    def add_landed(b):
        gk_ref[...] += gk_land[b - 1].astype(jnp.float32)
        gv_ref[...] += gv_land[b - 1].astype(jnp.float32)

    for b in range(1, back + 1):
        rows = slice((back - b) * tok, (back - b + 1) * tok)
        gk_send[b - 1] = key_sum[rows, :].astype(jnp.bfloat16)
        gv_send[b - 1] = value_sum[rows, :].astype(jnp.bfloat16)

        @pl.when((me >= b) & (odd == 0) if relay and b == 2 else (me >= b))
        def _():
            for copy in halo_out(b):
                copy.start()

    gk_ref[...] = key_sum[back * tok :, :]
    gv_ref[...] = value_sum[back * tok :, :]
    send_query_grads(parts - 1)
    own_gq = pltpu.make_async_copy(gq_buf.at[me], gq_ref.at[me], own_sem.at[7])
    own_gq.start()
    if relay:

        @pl.when((odd == 1) & (me >= 2))
        def _():
            for copy in halo_out(1):
                copy.wait_recv()
            gk_send[1] = (key_sum[:tok, :] + gk_land[0].astype(jnp.float32)).astype(jnp.bfloat16)
            gv_send[1] = (value_sum[:tok, :] + gv_land[0].astype(jnp.float32)).astype(jnp.bfloat16)
            for copy in halo_out(2):
                copy.start()
            for copy in halo_forward():
                copy.wait_send()

        @pl.when(odd == 0)
        def _():
            for copy in halo_out(1):
                copy.wait_recv()
            add_landed(1)

    for b in range(2 if relay else 1, back + 1):

        @pl.when(me + b < n)
        def _():
            for copy in halo_out(b):
                copy.wait_recv()
            add_landed(b)

    for b in range(1, back + 1):

        @pl.when(me >= b)
        def _():
            for copy in halo_out(b):
                copy.wait_send()

    own_att.wait()
    own_gq.wait()
    for offset in range(1, n):
        spread(g_ref, gbuf, g_ssem, g_rsem, offset).wait_send()
        for part in range(parts):
            spread_part(att_buf, att_ref, a_ssem, a_rsem, part, offset).wait()
            spread_part(gq_buf, gq_ref, gq_ssem, gq_rsem, part, offset).wait()


def widen(att_ref, gq_ref, gk_ref, gv_ref, att_out, gq_out, gk_out, gv_out):
    att_out[...] = att_ref[...].astype(jnp.float32)
    gq_out[...] = gq_ref[...].astype(jnp.float32)
    gk_out[...] = gk_ref[...]
    gv_out[...] = gv_ref[...]


def per_device(n, queries, keys, values, grad_out, lengths, send_order):
    tok, head_dim = keys.shape
    width = queries.shape[1]
    heads = width // head_dim
    group = tok // n
    longest = n * tok // 4
    back = min(n - 1, -(-(longest - 1) // tok))
    window = (back + 1) * tok
    flops = 2 * tok * heads * window * head_dim * 5
    vmem = pl.BlockSpec(memory_space=pltpu.VMEM)
    hbm = pl.BlockSpec(memory_space=pltpu.HBM)
    parts = math.gcd(heads, 2)
    vmem_limit = 62 * 1024 * 1024
    dma = pltpu.SemaphoreType.DMA
    att, gq, gk, gv = pl.pallas_call(
        functools.partial(kernel, n, back),
        out_shape=(
            jax.ShapeDtypeStruct((n, group, width), jnp.bfloat16),
            jax.ShapeDtypeStruct((n, group, width), jnp.bfloat16),
            jax.ShapeDtypeStruct((tok, head_dim), jnp.float32),
            jax.ShapeDtypeStruct((tok, head_dim), jnp.float32),
        ),
        in_specs=[hbm] * 6,
        out_specs=(hbm, hbm, vmem, vmem),
        scratch_shapes=[
            pltpu.VMEM((tok, width), jnp.bfloat16),
            pltpu.SMEM(lengths.shape, jnp.int32),
            pltpu.VMEM(send_order.shape, jnp.int32),
            pltpu.VMEM((window, head_dim), jnp.bfloat16),
            pltpu.VMEM((window, head_dim), jnp.bfloat16),
            pltpu.VMEM((n, group, width), jnp.bfloat16),
            pltpu.VMEM((n, group, width), jnp.bfloat16),
            pltpu.VMEM((n, group, width), jnp.bfloat16),
            pltpu.VMEM((window, tok), jnp.float32),
            pltpu.VMEM((heads, window, tok), jnp.float32),
            pltpu.VMEM((back, tok, head_dim), jnp.bfloat16),
            pltpu.VMEM((back, tok, head_dim), jnp.bfloat16),
            pltpu.VMEM((back, tok, head_dim), jnp.bfloat16),
            pltpu.VMEM((back, tok, head_dim), jnp.bfloat16),
            dma((2, back)),
            dma((2, back)),
            dma((n,)),
            dma((n,)),
            dma((parts, n)),
            dma((parts, n)),
            dma((parts, n)),
            dma((parts, n)),
            dma((2, back)),
            dma((2, back)),
            dma((8,)),
        ],
        compiler_params=pltpu.CompilerParams(
            collective_id=0, has_side_effects=True, vmem_limit_bytes=vmem_limit
        ),
        cost_estimate=pl.CostEstimate(
            flops=flops, bytes_accessed=6 * tok * width, transcendentals=tok * heads * window
        ),
    )(queries, keys, values, grad_out.reshape(n, group, width), lengths, send_order)
    steps = 2
    wide = pl.BlockSpec((n // steps, group, width), lambda i: (i, 0, 0))
    narrow = pl.BlockSpec((tok // steps, head_dim), lambda i: (i, 0))
    blocks = (wide, wide, narrow, narrow)
    att, gq, gk, gv = pl.pallas_call(
        widen,
        out_shape=(
            jax.ShapeDtypeStruct((n, group, width), jnp.float32),
            jax.ShapeDtypeStruct((n, group, width), jnp.float32),
            jax.ShapeDtypeStruct((tok, head_dim), jnp.float32),
            jax.ShapeDtypeStruct((tok, head_dim), jnp.float32),
        ),
        grid=(steps,),
        in_specs=blocks,
        out_specs=blocks,
        compiler_params=pltpu.CompilerParams(vmem_limit_bytes=vmem_limit),
    )(att, gq, gk, gv)
    return (att.reshape(tok, width), gq.reshape(tok, width), gk, gv)


def solution(mesh):
    placed = (P("seq", "head"), P("seq", "head"), P("seq", "head"), P("seq", "head"), P(), P())
    return jax.shard_map(
        functools.partial(per_device, mesh.shape["seq"]),
        mesh=mesh,
        in_specs=placed,
        out_specs=(P("seq", "head"), P("seq", "head"), P("seq", "head"), P("seq", "head")),
        check_vma=False,
    )
```

```python
import functools
import math

import jax
import jax.numpy as jnp
from jax import lax
from jax.experimental import pallas as pl
from jax.experimental.pallas import tpu as pltpu
from jax.sharding import PartitionSpec as P

MESH = pl.DeviceIdType.MESH
masked_value = -1e30


def dot_nt(a, b):
    return lax.dot_general(a, b, (((1,), (1,)), ((), ())), preferred_element_type=jnp.float32)


def dot_nn(a, b):
    return jnp.dot(a, b, preferred_element_type=jnp.float32)


def kernel(
    n,
    back,
    q_hbm,
    k_ref,
    v_ref,
    g_ref,
    len_hbm,
    order_hbm,
    att_ref,
    gq_ref,
    gk_ref,
    gv_ref,
    q_ref,
    len_ref,
    order_ref,
    kwin,
    vwin,
    gbuf,
    att_buf,
    gq_buf,
    bias,
    weights,
    gk_send,
    gv_send,
    gk_land,
    gv_land,
    kv_ssem,
    kv_rsem,
    g_ssem,
    g_rsem,
    a_ssem,
    a_rsem,
    gq_ssem,
    gq_rsem,
    gkv_ssem,
    gkv_rsem,
    own_sem,
):
    me = lax.axis_index("seq")
    tok, head_dim = k_ref.shape
    group = tok // n
    parts = a_ssem.shape[0]
    heads = q_ref.shape[1] // head_dim
    window = (back + 1) * tok
    scale = 1.0 / math.sqrt(head_dim)

    def peer(offset):
        return lax.rem(me + offset, n)

    def remote(src, dst, ssem, rsem, target):
        return pltpu.make_async_remote_copy(
            src_ref=src,
            dst_ref=dst,
            send_sem=ssem,
            recv_sem=rsem,
            device_id={"seq": target},
            device_id_type=MESH,
        )

    relay = back == 2 and n % 2 == 0
    odd = lax.rem(me, 2)
    partner = me + 1 - 2 * odd

    def halo_in(b):
        rows = pl.ds((back - b) * tok, tok)
        target = partner if relay and b == 1 else peer(b)
        return (
            remote(k_ref, kwin.at[rows], kv_ssem.at[0, b - 1], kv_rsem.at[0, b - 1], target),
            remote(v_ref, vwin.at[rows], kv_ssem.at[1, b - 1], kv_rsem.at[1, b - 1], target),
        )

    def halo_forward():
        old, new = pl.ds(0, tok), pl.ds(tok, tok)
        return (
            remote(kwin.at[old], kwin.at[new], kv_ssem.at[0, 0], kv_rsem.at[0, 0], partner),
            remote(vwin.at[old], vwin.at[new], kv_ssem.at[1, 0], kv_rsem.at[1, 0], partner),
        )

    def halo_out(b):
        target = partner if relay and b == 1 else peer(n - b)
        return (
            remote(
                gk_send.at[b - 1],
                gk_land.at[b - 1],
                gkv_ssem.at[0, b - 1],
                gkv_rsem.at[0, b - 1],
                target,
            ),
            remote(
                gv_send.at[b - 1],
                gv_land.at[b - 1],
                gkv_ssem.at[1, b - 1],
                gkv_rsem.at[1, b - 1],
                target,
            ),
        )

    def spread(src, dst, ssem, rsem, offset):
        target = peer(offset)
        return remote(src.at[target], dst.at[me], ssem.at[offset], rsem.at[offset], target)

    def spread_part(src, dst, ssem, rsem, part, offset):
        target = peer(offset)
        return remote(
            src.at[part, target],
            dst.at[part, me],
            ssem.at[part, offset],
            rsem.at[part, offset],
            target,
        )

    far_first = sorted(range(1, n), key=lambda offset: abs(offset - n // 2))

    barrier = pltpu.get_barrier_semaphore()
    for offset in range(1, n):
        pl.semaphore_signal(
            barrier, inc=1, device_id={"seq": peer(offset)}, device_id_type=MESH
        )

    own_rows = pl.ds(back * tok, tok)
    local = [
        pltpu.make_async_copy(order_hbm, order_ref, own_sem.at[0]),
        pltpu.make_async_copy(len_hbm, len_ref, own_sem.at[1]),
        pltpu.make_async_copy(q_hbm, q_ref, own_sem.at[2]),
        pltpu.make_async_copy(k_ref, kwin.at[own_rows], own_sem.at[3]),
        pltpu.make_async_copy(v_ref, vwin.at[own_rows], own_sem.at[4]),
        pltpu.make_async_copy(g_ref.at[me], gbuf.at[me], own_sem.at[5]),
    ]
    for copy in local:
        copy.start()
    for b in range(1, back + 1):

        @pl.when(me < b)
        def _():
            kwin[(back - b) * tok : (back - b + 1) * tok, :] = jnp.zeros((tok, head_dim), kwin.dtype)
            vwin[(back - b) * tok : (back - b + 1) * tok, :] = jnp.zeros((tok, head_dim), vwin.dtype)

    pl.semaphore_wait(barrier, n - 1)
    for b in range(back, 0, -1):

        @pl.when((odd == 0) if relay and b == 1 else (me + b < n))
        def _():
            for copy in halo_in(b):
                copy.start()

    for offset in far_first:
        spread(g_ref, gbuf, g_ssem, g_rsem, offset).start()

    for copy in local:
        copy.wait()

    order = order_ref[pl.ds(me, 1), :]
    one_hot = (lax.broadcasted_iota(jnp.int32, (tok, tok), 0) == order).astype(jnp.float32)
    picked = dot_nn(one_hot.T.astype(jnp.bfloat16), q_ref[...]).astype(jnp.bfloat16)
    query_pos = order + me * tok
    start = jnp.zeros_like(query_pos)
    bound = jnp.int32(0)
    for d in range(len_ref.shape[0]):
        bound = bound + len_ref[d]
        start = jnp.where(query_pos >= bound, bound, start)
    key_pos = lax.broadcasted_iota(jnp.int32, (window, tok), 0) + (me - back) * tok
    allowed = (key_pos >= start) & (key_pos <= query_pos)
    bias[...] = jnp.where(allowed, 0.0, masked_value)

    if relay:

        @pl.when(me >= 2)
        def _():
            for copy, onward in zip(halo_in(2), halo_forward()):
                copy.wait_recv()

                @pl.when(odd == 1)
                def _():
                    onward.start()

    for b in range(1, 2 if relay else back + 1):

        @pl.when(me >= b)
        def _():
            for copy in halo_in(b):
                copy.wait_recv()

    key_all = kwin[...]
    value_all = vwin[...]
    key_t = key_all.astype(jnp.float32).T.astype(jnp.bfloat16)
    value_t = value_all.astype(jnp.float32).T.astype(jnp.bfloat16)
    exponent = scale * math.log2(math.e)

    att_cols = []
    for h in range(heads):
        cols = slice(h * head_dim, (h + 1) * head_dim)
        scores = dot_nt(key_all, picked[:, cols]) + bias[...]
        row_max = jnp.max(scores, axis=0, keepdims=True)
        exps = jnp.exp2((scores - row_max) * exponent)
        weight = exps * (1.0 / jnp.sum(exps, axis=0, keepdims=True))
        weights[h] = weight
        att_t = dot_nn(value_t, weight.astype(jnp.bfloat16))
        att_low = att_t.T
        att_cols.append(att_t.astype(jnp.bfloat16).astype(jnp.float32))
        part, place = divmod(h, heads // parts)
        part_cols = slice(place * head_dim, (place + 1) * head_dim)
        att_buf[part, :, :, part_cols] = att_low.reshape(n, group, head_dim).astype(jnp.bfloat16)
        if (h + 1) * parts % heads == 0:
            for offset in far_first:
                spread_part(att_buf, att_ref, a_ssem, a_rsem, part, offset).start()
    own_att = pltpu.make_async_copy(att_buf.at[:, me], att_ref.at[:, me], own_sem.at[6])
    own_att.start()

    for offset in range(1, n):
        spread(g_ref, gbuf, g_ssem, g_rsem, offset).wait_recv()

    def send_query_grads(part):
        for h in range(part * heads // parts, (part + 1) * heads // parts):
            query_grad = (dot_nn(key_t, score_grads[h]) * scale).T
            place = h % (heads // parts)
            part_cols = slice(place * head_dim, (place + 1) * head_dim)
            gq_buf[part, :, :, part_cols] = query_grad.reshape(n, group, head_dim).astype(jnp.bfloat16)
        for offset in far_first:
            spread_part(gq_buf, gq_ref, gq_ssem, gq_rsem, part, offset).start()

    score_grads = []
    for h in range(heads):
        cols = slice(h * head_dim, (h + 1) * head_dim)
        grad_float = gbuf[:, :, cols].astype(jnp.float32).reshape(tok, head_dim)
        grad = grad_float.astype(jnp.bfloat16)
        out_dot = jnp.sum(grad_float.T * att_cols[h], axis=0, keepdims=True)
        weight = weights[h]
        score_grads.append((weight * (dot_nt(value_all, grad) - out_dot)).astype(jnp.bfloat16))
        key_term = dot_nn(score_grads[h], picked[:, cols])
        value_term = dot_nn(weight.astype(jnp.bfloat16), grad)
        key_sum = key_term if h == 0 else key_sum + key_term
        value_sum = value_term if h == 0 else value_sum + value_term
        if h + 1 < heads and (h + 1) * parts % heads == 0:
            send_query_grads((h + 1) * parts // heads - 1)

    key_sum = key_sum * scale

    def add_landed(b):
        gk_ref[...] += gk_land[b - 1].astype(jnp.float32)
        gv_ref[...] += gv_land[b - 1].astype(jnp.float32)

    for b in range(1, back + 1):
        rows = slice((back - b) * tok, (back - b + 1) * tok)
        gk_send[b - 1] = key_sum[rows, :].astype(jnp.bfloat16)
        gv_send[b - 1] = value_sum[rows, :].astype(jnp.bfloat16)

        @pl.when((me >= b) & (odd == 0) if relay and b == 2 else (me >= b))
        def _():
            for copy in halo_out(b):
                copy.start()

    gk_ref[...] = key_sum[back * tok :, :]
    gv_ref[...] = value_sum[back * tok :, :]
    send_query_grads(parts - 1)
    own_gq = pltpu.make_async_copy(gq_buf.at[:, me], gq_ref.at[:, me], own_sem.at[7])
    own_gq.start()
    if relay:

        @pl.when((odd == 1) & (me >= 2))
        def _():
            for copy in halo_out(1):
                copy.wait_recv()
            gk_send[1] = (key_sum[:tok, :] + gk_land[0].astype(jnp.float32)).astype(jnp.bfloat16)
            gv_send[1] = (value_sum[:tok, :] + gv_land[0].astype(jnp.float32)).astype(jnp.bfloat16)
            for copy in halo_out(2):
                copy.start()
            for copy in halo_forward():
                copy.wait_send()

        @pl.when(odd == 0)
        def _():
            for copy in halo_out(1):
                copy.wait_recv()
            add_landed(1)

    for b in range(2 if relay else 1, back + 1):

        @pl.when(me + b < n)
        def _():
            for copy in halo_out(b):
                copy.wait_recv()
            add_landed(b)

    for b in range(1, back + 1):

        @pl.when(me >= b)
        def _():
            for copy in halo_out(b):
                copy.wait_send()

    for b in range(1, back + 1):

        @pl.when((odd == 0) if relay and b == 1 else (me + b < n))
        def _():
            for copy in halo_in(b):
                copy.wait_send()

    own_att.wait()
    own_gq.wait()
    for offset in range(1, n):
        spread(g_ref, gbuf, g_ssem, g_rsem, offset).wait_send()
        for part in range(parts):
            spread_part(att_buf, att_ref, a_ssem, a_rsem, part, offset).wait()
            spread_part(gq_buf, gq_ref, gq_ssem, gq_rsem, part, offset).wait()


def widen(att_ref, gq_ref, gk_ref, gv_ref, att_out, gq_out, gk_out, gv_out):
    parts, _, _, width = att_ref.shape
    for part in range(parts):
        cols = slice(part * width, (part + 1) * width)
        att_out[:, :, cols] = att_ref[part].astype(jnp.float32)
        gq_out[:, :, cols] = gq_ref[part].astype(jnp.float32)
    gk_out[...] = gk_ref[...]
    gv_out[...] = gv_ref[...]


def per_device(n, queries, keys, values, grad_out, lengths, send_order):
    tok, head_dim = keys.shape
    width = queries.shape[1]
    heads = width // head_dim
    group = tok // n
    longest = n * tok // 4
    back = min(n - 1, -(-(longest - 1) // tok))
    window = (back + 1) * tok
    flops = 2 * tok * heads * window * head_dim * 5
    vmem = pl.BlockSpec(memory_space=pltpu.VMEM)
    hbm = pl.BlockSpec(memory_space=pltpu.HBM)
    parts = math.gcd(heads, 2)
    vmem_limit = 62 * 1024 * 1024
    dma = pltpu.SemaphoreType.DMA
    att, gq, gk, gv = pl.pallas_call(
        functools.partial(kernel, n, back),
        out_shape=(
            jax.ShapeDtypeStruct((parts, n, group, width // parts), jnp.bfloat16),
            jax.ShapeDtypeStruct((parts, n, group, width // parts), jnp.bfloat16),
            jax.ShapeDtypeStruct((tok, head_dim), jnp.float32),
            jax.ShapeDtypeStruct((tok, head_dim), jnp.float32),
        ),
        in_specs=[hbm] * 6,
        out_specs=(hbm, hbm, vmem, vmem),
        scratch_shapes=[
            pltpu.VMEM((tok, width), jnp.bfloat16),
            pltpu.SMEM(lengths.shape, jnp.int32),
            pltpu.VMEM(send_order.shape, jnp.int32),
            pltpu.VMEM((window, head_dim), jnp.bfloat16),
            pltpu.VMEM((window, head_dim), jnp.bfloat16),
            pltpu.VMEM((n, group, width), jnp.bfloat16),
            pltpu.VMEM((parts, n, group, width // parts), jnp.bfloat16),
            pltpu.VMEM((parts, n, group, width // parts), jnp.bfloat16),
            pltpu.VMEM((window, tok), jnp.float32),
            pltpu.VMEM((heads, window, tok), jnp.float32),
            pltpu.VMEM((back, tok, head_dim), jnp.bfloat16),
            pltpu.VMEM((back, tok, head_dim), jnp.bfloat16),
            pltpu.VMEM((back, tok, head_dim), jnp.bfloat16),
            pltpu.VMEM((back, tok, head_dim), jnp.bfloat16),
            dma((2, back)),
            dma((2, back)),
            dma((n,)),
            dma((n,)),
            dma((parts, n)),
            dma((parts, n)),
            dma((parts, n)),
            dma((parts, n)),
            dma((2, back)),
            dma((2, back)),
            dma((8,)),
        ],
        compiler_params=pltpu.CompilerParams(
            collective_id=0, has_side_effects=True, vmem_limit_bytes=vmem_limit
        ),
        cost_estimate=pl.CostEstimate(
            flops=flops, bytes_accessed=6 * tok * width, transcendentals=tok * heads * window
        ),
    )(queries, keys, values, grad_out.reshape(n, group, width), lengths, send_order)
    steps = 2
    wide = pl.BlockSpec((n // steps, group, width), lambda i: (i, 0, 0))
    narrow = pl.BlockSpec((tok // steps, head_dim), lambda i: (i, 0))
    halves = pl.BlockSpec((parts, n // steps, group, width // parts), lambda i: (0, i, 0, 0))
    att, gq, gk, gv = pl.pallas_call(
        widen,
        out_shape=(
            jax.ShapeDtypeStruct((n, group, width), jnp.float32),
            jax.ShapeDtypeStruct((n, group, width), jnp.float32),
            jax.ShapeDtypeStruct((tok, head_dim), jnp.float32),
            jax.ShapeDtypeStruct((tok, head_dim), jnp.float32),
        ),
        grid=(steps,),
        in_specs=(halves, halves, narrow, narrow),
        out_specs=(wide, wide, narrow, narrow),
        compiler_params=pltpu.CompilerParams(vmem_limit_bytes=vmem_limit),
    )(att, gq, gk, gv)
    return (att.reshape(tok, width), gq.reshape(tok, width), gk, gv)


def solution(mesh):
    placed = (P("seq", "head"), P("seq", "head"), P("seq", "head"), P("seq", "head"), P(), P())
    return jax.shard_map(
        functools.partial(per_device, mesh.shape["seq"]),
        mesh=mesh,
        in_specs=placed,
        out_specs=(P("seq", "head"), P("seq", "head"), P("seq", "head"), P("seq", "head")),
        check_vma=False,
    )
```

```python
import functools
import math

import jax
import jax.numpy as jnp
from jax import lax
from jax.experimental import pallas as pl
from jax.experimental.pallas import tpu as pltpu
from jax.sharding import PartitionSpec as P

MESH = pl.DeviceIdType.MESH
masked_value = -1e30


def dot_nt(a, b):
    return lax.dot_general(a, b, (((1,), (1,)), ((), ())), preferred_element_type=jnp.float32)


def dot_nn(a, b):
    return jnp.dot(a, b, preferred_element_type=jnp.float32)


def kernel(
    n,
    back,
    q_hbm,
    k_ref,
    v_ref,
    g_ref,
    len_hbm,
    order_hbm,
    att_ref,
    gq_ref,
    gk_ref,
    gv_ref,
    q_ref,
    len_ref,
    order_ref,
    kwin,
    vwin,
    gbuf,
    att_buf,
    gq_buf,
    bias,
    weights,
    gk_send,
    gv_send,
    gk_land,
    gv_land,
    kv_ssem,
    kv_rsem,
    g_ssem,
    g_rsem,
    a_ssem,
    a_rsem,
    gq_ssem,
    gq_rsem,
    gkv_ssem,
    gkv_rsem,
    own_sem,
):
    me = lax.axis_index("seq")
    tok, head_dim = k_ref.shape
    group = tok // n
    parts = a_ssem.shape[0]
    heads = q_ref.shape[1] // head_dim
    window = (back + 1) * tok
    scale = 1.0 / math.sqrt(head_dim)

    def peer(offset):
        return lax.rem(me + offset, n)

    def remote(src, dst, ssem, rsem, target):
        return pltpu.make_async_remote_copy(
            src_ref=src,
            dst_ref=dst,
            send_sem=ssem,
            recv_sem=rsem,
            device_id={"seq": target},
            device_id_type=MESH,
        )

    relay = back == 2 and n % 2 == 0
    odd = lax.rem(me, 2)
    partner = me + 1 - 2 * odd

    def halo_in(b):
        rows = pl.ds((back - b) * tok, tok)
        target = partner if relay and b == 1 else peer(b)
        return (
            remote(k_ref, kwin.at[rows], kv_ssem.at[0, b - 1], kv_rsem.at[0, b - 1], target),
            remote(v_ref, vwin.at[rows], kv_ssem.at[1, b - 1], kv_rsem.at[1, b - 1], target),
        )

    def halo_forward():
        old, new = pl.ds(0, tok), pl.ds(tok, tok)
        return (
            remote(kwin.at[old], kwin.at[new], kv_ssem.at[0, 0], kv_rsem.at[0, 0], partner),
            remote(vwin.at[old], vwin.at[new], kv_ssem.at[1, 0], kv_rsem.at[1, 0], partner),
        )

    def halo_out(b):
        target = partner if relay and b == 1 else peer(n - b)
        return (
            remote(
                gk_send.at[b - 1],
                gk_land.at[b - 1],
                gkv_ssem.at[0, b - 1],
                gkv_rsem.at[0, b - 1],
                target,
            ),
            remote(
                gv_send.at[b - 1],
                gv_land.at[b - 1],
                gkv_ssem.at[1, b - 1],
                gkv_rsem.at[1, b - 1],
                target,
            ),
        )

    def spread(src, dst, ssem, rsem, offset):
        target = peer(offset)
        return remote(src.at[target], dst.at[me], ssem.at[offset], rsem.at[offset], target)

    def spread_part(src, dst, ssem, rsem, part, offset):
        target = peer(offset)
        return remote(
            src.at[part, target],
            dst.at[part, me],
            ssem.at[part, offset],
            rsem.at[part, offset],
            target,
        )

    far_first = sorted(range(1, n), key=lambda offset: abs(offset - n // 2))

    barrier = pltpu.get_barrier_semaphore()
    for offset in range(1, n):
        pl.semaphore_signal(
            barrier, inc=1, device_id={"seq": peer(offset)}, device_id_type=MESH
        )

    own_rows = pl.ds(back * tok, tok)
    local = [
        pltpu.make_async_copy(order_hbm, order_ref, own_sem.at[0]),
        pltpu.make_async_copy(len_hbm, len_ref, own_sem.at[1]),
        pltpu.make_async_copy(q_hbm, q_ref, own_sem.at[2]),
        pltpu.make_async_copy(k_ref, kwin.at[own_rows], own_sem.at[3]),
        pltpu.make_async_copy(v_ref, vwin.at[own_rows], own_sem.at[4]),
        pltpu.make_async_copy(g_ref.at[me], gbuf.at[me], own_sem.at[5]),
    ]
    for copy in local:
        copy.start()
    for b in range(1, back + 1):

        @pl.when(me < b)
        def _():
            kwin[(back - b) * tok : (back - b + 1) * tok, :] = jnp.zeros((tok, head_dim), kwin.dtype)
            vwin[(back - b) * tok : (back - b + 1) * tok, :] = jnp.zeros((tok, head_dim), vwin.dtype)

    pl.semaphore_wait(barrier, n - 1)
    for b in range(back, 0, -1):

        @pl.when((odd == 0) if relay and b == 1 else (me + b < n))
        def _():
            for copy in halo_in(b):
                copy.start()

    for offset in far_first:
        spread(g_ref, gbuf, g_ssem, g_rsem, offset).start()

    for copy in local:
        copy.wait()

    order = order_ref[pl.ds(me, 1), :]
    one_hot = (lax.broadcasted_iota(jnp.int32, (tok, tok), 0) == order).astype(jnp.float32)
    picked = dot_nn(one_hot.T.astype(jnp.bfloat16), q_ref[...]).astype(jnp.bfloat16)
    query_pos = order + me * tok
    start = jnp.zeros_like(query_pos)
    bound = jnp.int32(0)
    for d in range(len_ref.shape[0]):
        bound = bound + len_ref[d]
        start = jnp.where(query_pos >= bound, bound, start)
    key_pos = lax.broadcasted_iota(jnp.int32, (window, tok), 0) + (me - back) * tok
    allowed = (key_pos >= start) & (key_pos <= query_pos)
    bias[...] = jnp.where(allowed, 0.0, masked_value)

    def score_rows(b):
        rows = slice((back - b) * tok, (back - b + 1) * tok)
        block = kwin[rows, :]
        for h in range(heads):
            cols = slice(h * head_dim, (h + 1) * head_dim)
            weights[h, rows, :] = dot_nt(block, picked[:, cols]) + bias[rows, :]
        return vwin[rows, :].astype(jnp.float32).T.astype(jnp.bfloat16)

    value_blocks = {0: score_rows(0)}
    if relay:

        @pl.when(me >= 2)
        def _():
            for copy, onward in zip(halo_in(2), halo_forward()):
                copy.wait_recv()

                @pl.when(odd == 1)
                def _():
                    onward.start()

        value_blocks[2] = score_rows(2)

    for b in range(1, 2 if relay else back + 1):

        @pl.when(me >= b)
        def _():
            for copy in halo_in(b):
                copy.wait_recv()

        value_blocks[b] = score_rows(b)

    value_t = jnp.concatenate([value_blocks[b] for b in range(back, -1, -1)], axis=1)
    exponent = scale * math.log2(math.e)

    att_cols = []
    for h in range(heads):
        scores = weights[h]
        row_max = jnp.max(scores, axis=0, keepdims=True)
        exps = jnp.exp2((scores - row_max) * exponent)
        weight = exps * (1.0 / jnp.sum(exps, axis=0, keepdims=True))
        weights[h] = weight
        att_t = dot_nn(value_t, weight.astype(jnp.bfloat16))
        att_low = att_t.T
        att_cols.append(att_t.astype(jnp.bfloat16).astype(jnp.float32))
        part, place = divmod(h, heads // parts)
        part_cols = slice(place * head_dim, (place + 1) * head_dim)
        att_buf[part, :, :, part_cols] = att_low.reshape(n, group, head_dim).astype(jnp.bfloat16)
        if (h + 1) * parts % heads == 0:
            for offset in far_first:
                spread_part(att_buf, att_ref, a_ssem, a_rsem, part, offset).start()
    own_att = pltpu.make_async_copy(att_buf.at[:, me], att_ref.at[:, me], own_sem.at[6])
    own_att.start()
    key_t = kwin[...].astype(jnp.float32).T.astype(jnp.bfloat16)
    value_all = vwin[...]

    for offset in range(1, n):
        spread(g_ref, gbuf, g_ssem, g_rsem, offset).wait_recv()

    def send_query_grads(part):
        for h in range(part * heads // parts, (part + 1) * heads // parts):
            query_grad = (dot_nn(key_t, score_grads[h]) * scale).T
            place = h % (heads // parts)
            part_cols = slice(place * head_dim, (place + 1) * head_dim)
            gq_buf[part, :, :, part_cols] = query_grad.reshape(n, group, head_dim).astype(jnp.bfloat16)
        for offset in far_first:
            spread_part(gq_buf, gq_ref, gq_ssem, gq_rsem, part, offset).start()

    score_grads = []
    for h in range(heads):
        cols = slice(h * head_dim, (h + 1) * head_dim)
        grad_float = gbuf[:, :, cols].astype(jnp.float32).reshape(tok, head_dim)
        grad = grad_float.astype(jnp.bfloat16)
        out_dot = jnp.sum(grad_float.T * att_cols[h], axis=0, keepdims=True)
        weight = weights[h]
        score_grads.append((weight * (dot_nt(value_all, grad) - out_dot)).astype(jnp.bfloat16))
        key_term = dot_nn(score_grads[h], picked[:, cols])
        value_term = dot_nn(weight.astype(jnp.bfloat16), grad)
        key_sum = key_term if h == 0 else key_sum + key_term
        value_sum = value_term if h == 0 else value_sum + value_term
        if h + 1 < heads and (h + 1) * parts % heads == 0:
            send_query_grads((h + 1) * parts // heads - 1)

    key_sum = key_sum * scale

    def add_landed(b):
        gk_ref[...] += gk_land[b - 1].astype(jnp.float32)
        gv_ref[...] += gv_land[b - 1].astype(jnp.float32)

    for b in range(1, back + 1):
        rows = slice((back - b) * tok, (back - b + 1) * tok)
        gk_send[b - 1] = key_sum[rows, :].astype(jnp.bfloat16)
        gv_send[b - 1] = value_sum[rows, :].astype(jnp.bfloat16)

        @pl.when((me >= b) & (odd == 0) if relay and b == 2 else (me >= b))
        def _():
            for copy in halo_out(b):
                copy.start()

    gk_ref[...] = key_sum[back * tok :, :]
    gv_ref[...] = value_sum[back * tok :, :]
    send_query_grads(parts - 1)
    own_gq = pltpu.make_async_copy(gq_buf.at[:, me], gq_ref.at[:, me], own_sem.at[7])
    own_gq.start()
    if relay:

        @pl.when((odd == 1) & (me >= 2))
        def _():
            for copy in halo_out(1):
                copy.wait_recv()
            gk_send[1] = (key_sum[:tok, :] + gk_land[0].astype(jnp.float32)).astype(jnp.bfloat16)
            gv_send[1] = (value_sum[:tok, :] + gv_land[0].astype(jnp.float32)).astype(jnp.bfloat16)
            for copy in halo_out(2):
                copy.start()
            for copy in halo_forward():
                copy.wait_send()

        @pl.when(odd == 0)
        def _():
            for copy in halo_out(1):
                copy.wait_recv()
            add_landed(1)

    for b in range(2 if relay else 1, back + 1):

        @pl.when(me + b < n)
        def _():
            for copy in halo_out(b):
                copy.wait_recv()
            add_landed(b)

    for b in range(1, back + 1):

        @pl.when(me >= b)
        def _():
            for copy in halo_out(b):
                copy.wait_send()

    for b in range(1, back + 1):

        @pl.when((odd == 0) if relay and b == 1 else (me + b < n))
        def _():
            for copy in halo_in(b):
                copy.wait_send()

    own_att.wait()
    own_gq.wait()
    for offset in range(1, n):
        spread(g_ref, gbuf, g_ssem, g_rsem, offset).wait_send()
        for part in range(parts):
            spread_part(att_buf, att_ref, a_ssem, a_rsem, part, offset).wait()
            spread_part(gq_buf, gq_ref, gq_ssem, gq_rsem, part, offset).wait()


def widen(att_ref, gq_ref, gk_ref, gv_ref, att_out, gq_out, gk_out, gv_out):
    parts, _, _, width = att_ref.shape
    for part in range(parts):
        cols = slice(part * width, (part + 1) * width)
        att_out[:, :, cols] = att_ref[part].astype(jnp.float32)
        gq_out[:, :, cols] = gq_ref[part].astype(jnp.float32)
    gk_out[...] = gk_ref[...]
    gv_out[...] = gv_ref[...]


def per_device(n, queries, keys, values, grad_out, lengths, send_order):
    tok, head_dim = keys.shape
    width = queries.shape[1]
    heads = width // head_dim
    group = tok // n
    longest = n * tok // 4
    back = min(n - 1, -(-(longest - 1) // tok))
    window = (back + 1) * tok
    flops = 2 * tok * heads * window * head_dim * 5
    vmem = pl.BlockSpec(memory_space=pltpu.VMEM)
    hbm = pl.BlockSpec(memory_space=pltpu.HBM)
    parts = math.gcd(heads, 2)
    vmem_limit = 62 * 1024 * 1024
    dma = pltpu.SemaphoreType.DMA
    att, gq, gk, gv = pl.pallas_call(
        functools.partial(kernel, n, back),
        out_shape=(
            jax.ShapeDtypeStruct((parts, n, group, width // parts), jnp.bfloat16),
            jax.ShapeDtypeStruct((parts, n, group, width // parts), jnp.bfloat16),
            jax.ShapeDtypeStruct((tok, head_dim), jnp.float32),
            jax.ShapeDtypeStruct((tok, head_dim), jnp.float32),
        ),
        in_specs=[hbm] * 6,
        out_specs=(hbm, hbm, vmem, vmem),
        scratch_shapes=[
            pltpu.VMEM((tok, width), jnp.bfloat16),
            pltpu.SMEM(lengths.shape, jnp.int32),
            pltpu.VMEM(send_order.shape, jnp.int32),
            pltpu.VMEM((window, head_dim), jnp.bfloat16),
            pltpu.VMEM((window, head_dim), jnp.bfloat16),
            pltpu.VMEM((n, group, width), jnp.bfloat16),
            pltpu.VMEM((parts, n, group, width // parts), jnp.bfloat16),
            pltpu.VMEM((parts, n, group, width // parts), jnp.bfloat16),
            pltpu.VMEM((window, tok), jnp.float32),
            pltpu.VMEM((heads, window, tok), jnp.float32),
            pltpu.VMEM((back, tok, head_dim), jnp.bfloat16),
            pltpu.VMEM((back, tok, head_dim), jnp.bfloat16),
            pltpu.VMEM((back, tok, head_dim), jnp.bfloat16),
            pltpu.VMEM((back, tok, head_dim), jnp.bfloat16),
            dma((2, back)),
            dma((2, back)),
            dma((n,)),
            dma((n,)),
            dma((parts, n)),
            dma((parts, n)),
            dma((parts, n)),
            dma((parts, n)),
            dma((2, back)),
            dma((2, back)),
            dma((8,)),
        ],
        compiler_params=pltpu.CompilerParams(
            collective_id=0, has_side_effects=True, vmem_limit_bytes=vmem_limit
        ),
        cost_estimate=pl.CostEstimate(
            flops=flops, bytes_accessed=6 * tok * width, transcendentals=tok * heads * window
        ),
    )(queries, keys, values, grad_out.reshape(n, group, width), lengths, send_order)
    steps = 2
    wide = pl.BlockSpec((n // steps, group, width), lambda i: (i, 0, 0))
    narrow = pl.BlockSpec((tok // steps, head_dim), lambda i: (i, 0))
    halves = pl.BlockSpec((parts, n // steps, group, width // parts), lambda i: (0, i, 0, 0))
    att, gq, gk, gv = pl.pallas_call(
        widen,
        out_shape=(
            jax.ShapeDtypeStruct((n, group, width), jnp.float32),
            jax.ShapeDtypeStruct((n, group, width), jnp.float32),
            jax.ShapeDtypeStruct((tok, head_dim), jnp.float32),
            jax.ShapeDtypeStruct((tok, head_dim), jnp.float32),
        ),
        grid=(steps,),
        in_specs=(halves, halves, narrow, narrow),
        out_specs=(wide, wide, narrow, narrow),
        compiler_params=pltpu.CompilerParams(vmem_limit_bytes=vmem_limit),
    )(att, gq, gk, gv)
    return (att.reshape(tok, width), gq.reshape(tok, width), gk, gv)


def solution(mesh):
    placed = (P("seq", "head"), P("seq", "head"), P("seq", "head"), P("seq", "head"), P(), P())
    return jax.shard_map(
        functools.partial(per_device, mesh.shape["seq"]),
        mesh=mesh,
        in_specs=placed,
        out_specs=(P("seq", "head"), P("seq", "head"), P("seq", "head"), P("seq", "head")),
        check_vma=False,
    )
```
